256 devices in a mesh: prow: 32 (over y, x, core), pcol: 8 (over z).
Axes of the slice: x: 4, y: 4, z: 8, core: 2. Of those that a mesh axis runs over, the one named last changes fastest.
Arguments:
- right_side: bfloat16 [5, 256, 128, 256], P(None, ('prow', 'pcol')), may hold values from -6 to 6
- lower_inverse: bfloat16 [5, 256, 128, 128], P(None, ('prow', 'pcol')), may hold values from -1.5 to 1.5
- upper_inverse: bfloat16 [5, 256, 128, 128], P(None, ('prow', 'pcol')), may hold values from -1.5 to 1.5
- lower_blocks: bfloat16 [4, 256, 48, 128, 128], P(None, 'prow', 'pcol'), may hold values from -0.0546875 to 0.0546875
- lower_index: int32 [4, 256, 48], P(None, 'prow', 'pcol'), may hold values from 0 to 127, as said below
- upper_blocks: bfloat16 [4, 256, 48, 128, 128], P(None, 'prow', 'pcol'), may hold values from -0.0546875 to 0.0546875
- upper_index: int32 [4, 256, 48], P(None, 'prow', 'pcol'), may hold values from 32 to 159, as said below
Outputs:
- solution: bfloat16 [5, 256, 128, 256], P(None, ('prow', 'pcol'))
The draws below stay inside these ranges and needn't reach their ends.
Inputs may be any that keep to these rules, and one draw needn't show every extreme that they name: lower_index[l, m, j] names a supernode of a level below l + 1; numbers may repeat. upper_index[l, m, j] names a supernode of a level above l; numbers may repeat.
All inputs are finite; a program needn't handle non-finite values.
Results may differ from the reference program's by a relative error of at most 0.014.
Values may be sent and summed in bfloat16 or wider, within the bound.
No kernel may reach another device: no remote copies, remote signals or barrier semaphores. Data moves between devices by JAX's collectives and lax.ppermute only.
A program may use at most 128 MiB of HBM per device.

```python
import jax
import jax.numpy as jnp
from jax import lax

W = 128
NRHS = 256
NL = 5
NNZ = 6
SUP_DEV = 1
M = 256
N_PROW = 32
N_PCOL = 8


def assemble(offdiag, key):
    diagonal = jax.random.uniform(key, (NL, M, W, 1), jnp.float32, 0.5, 0.8)
    identity = (jnp.arange(W)[:, None] == jnp.arange(W)[None, :]).astype(jnp.float32)
    return (diagonal * identity + 0.4 * W ** (-0.5) * offdiag).astype(jnp.bfloat16)


def draw_lower_inverse(key, part):
    key = jax.random.fold_in(key, 11)
    first, second = jax.random.split(key)
    offdiag = jnp.clip(jax.random.normal(first, (NL, M, W, W), jnp.float32), -4.0, 4.0)
    return assemble(offdiag, second)


def draw_upper_inverse(key, part):
    key = jax.random.fold_in(key, 17)
    first, second = jax.random.split(key)
    offdiag = jnp.clip(jax.random.normal(first, (NL, M, W, W), jnp.float32), -4.0, 4.0)
    return assemble(offdiag, second)


def draw_lower_index(key, part):
    key = jax.random.fold_in(key, 23)
    first, second = jax.random.split(key)
    per_group = N_PROW * SUP_DEV
    shape = (NL - 1, M, N_PCOL * NNZ)
    ceiling = jnp.arange(1, NL, dtype=jnp.int32)[:, None, None]
    height = jax.random.randint(first, shape, 0, ceiling, dtype=jnp.int32)
    entry = jax.random.randint(second, shape, 0, per_group, dtype=jnp.int32)
    pointers = height * per_group + entry
    pointers = pointers.at[0, 0, 0].set(0)
    pointers = pointers.at[NL - 2, 0, N_PCOL * NNZ - 1].set((NL - 1) * per_group - 1)
    return pointers.astype(jnp.int32)


def draw_upper_index(key, part):
    key = jax.random.fold_in(key, 29)
    first, second = jax.random.split(key)
    per_group = N_PROW * SUP_DEV
    shape = (NL - 1, M, N_PCOL * NNZ)
    floor_level = jnp.arange(1, NL, dtype=jnp.int32)[:, None, None]
    height = jax.random.randint(first, shape, floor_level, NL, dtype=jnp.int32)
    entry = jax.random.randint(second, shape, 0, per_group, dtype=jnp.int32)
    pointers = height * per_group + entry
    pointers = pointers.at[0, 0, 0].set(per_group)
    pointers = pointers.at[0, 0, N_PCOL * NNZ - 1].set(NL * per_group - 1)
    return pointers.astype(jnp.int32)


def steps_of(own_key, shape, cuts, smallest, high):
    factor_of, own = 1.0, jax.random.fold_in(own_key, 6)
    for position, shards_of in cuts:
        heights = jnp.exp(jax.random.uniform(jax.random.fold_in(own, position), (shards_of,), jnp.float32, smallest / len(cuts), high / len(cuts)))
        factor_of = factor_of * jnp.repeat(heights, shape[position] // shards_of).reshape([-1 if axis == position else 1 for axis in range(len(shape))])
    return factor_of


def scatter_about(stream_key, shape, deviation, reach, cuts=(), kind=jnp.bfloat16):
    loudness = steps_of(stream_key, shape, cuts, -0.22, 0.18) if cuts else 1.0
    drawn = jax.random.normal(stream_key, shape, jnp.float32) * deviation * loudness
    return jnp.minimum(jnp.maximum(drawn, -reach), reach).astype(kind)


def setup_inputs(seed: int = 0) -> dict:
    splits = jax.random.split(jax.random.key(seed), 8)
    return {
        "right_side": scatter_about(splits[0], (NL, M, W, NRHS), 1.0, 6.0, ((1, 256),)),
        "lower_inverse": draw_lower_inverse(jax.random.fold_in(splits[7], 71), 0),
        "upper_inverse": draw_upper_inverse(jax.random.fold_in(splits[7], 71), 0),
        "lower_blocks": scatter_about(splits[3], (NL - 1, M, N_PCOL * NNZ, W, W), (2 * W * NNZ * N_PCOL) ** -0.5, 0.0546875, ((1, 32), (2, 8))),
        "lower_index": draw_lower_index(jax.random.fold_in(splits[7], 71), 0),
        "upper_blocks": scatter_about(splits[5], (NL - 1, M, N_PCOL * NNZ, W, W), (2 * W * NNZ * N_PCOL) ** -0.5, 0.0546875, ((1, 32), (2, 8))),
        "upper_index": draw_upper_index(jax.random.fold_in(splits[7], 71), 0),
    }


def node_ids(pointers):
    per_group = N_PROW * SUP_DEV
    height = pointers // per_group
    entry = pointers % per_group
    owner = (jnp.arange(N_PCOL * NNZ, dtype=jnp.int32) // NNZ)[None, :]
    node = ((entry // SUP_DEV) * N_PCOL + owner) * SUP_DEV + entry % SUP_DEV
    return (height * M + node).astype(jnp.int32)


def level_sums(blocks, pointers, stored):
    ids = node_ids(pointers)

    def one_row(item):
        block_row, id_row = item
        picked = jnp.take(stored, id_row, axis=0).astype(jnp.float32)
        return jnp.einsum("kvw,kwn->vn", block_row.astype(jnp.float32), picked)

    return lax.map(one_row, (blocks, ids))


def apply_inverse(inverse, remain):
    product = jnp.einsum("mvw,mwn->mvn", inverse.astype(jnp.float32), remain.astype(jnp.float32))
    return product.astype(jnp.bfloat16)


def reference(right_side, lower_inverse, upper_inverse, lower_blocks, lower_index, upper_blocks, upper_index):
    stored = jnp.zeros((NL * M, W, NRHS), jnp.bfloat16)
    forward = [apply_inverse(lower_inverse[0], right_side[0])]
    for height in range(1, NL):
        stored = stored.at[(height - 1) * M:height * M].set(forward[-1])
        totals = level_sums(lower_blocks[height - 1], lower_index[height - 1], stored)
        remain = (right_side[height].astype(jnp.float32) - totals).astype(jnp.bfloat16)
        forward.append(apply_inverse(lower_inverse[height], remain))
    stored = jnp.zeros((NL * M, W, NRHS), jnp.bfloat16)
    result = [forward[0]] * NL
    result[NL - 1] = apply_inverse(upper_inverse[NL - 1], forward[NL - 1])
    for height in range(NL - 2, -1, -1):
        stored = stored.at[(height + 1) * M:(height + 2) * M].set(result[height + 1])
        totals = level_sums(upper_blocks[height], upper_index[height], stored)
        remain = (forward[height].astype(jnp.float32) - totals).astype(jnp.bfloat16)
        result[height] = apply_inverse(upper_inverse[height], remain)
    return jnp.stack(result)
```

```python
import functools

import jax
import jax.numpy as jnp
from jax import lax
from jax.experimental import pallas as pl
from jax.experimental.pallas import tpu as pltpu
from jax.sharding import PartitionSpec as P

F32 = jnp.float32
BF16 = jnp.bfloat16


def first_kernel(own_inverse, mate_inverse, own_side, mate_side, out):
    for slot, (inverse, side) in enumerate(((own_inverse, own_side), (mate_inverse, mate_side))):
        out[slot] = jnp.dot(inverse[0], side[0], preferred_element_type=F32).astype(BF16)


def solve_kernel(terms, own_inverse, mate_inverse, own_side, mate_side, out):
    for slot, (inverse, side) in enumerate(((own_inverse, own_side), (mate_inverse, mate_side))):
        total = terms[0, slot].astype(F32)
        for source in range(1, terms.shape[0]):
            total += terms[source, slot].astype(F32)
        remain = (side[0].astype(F32) - total).astype(BF16)
        out[slot] = jnp.dot(inverse[0], remain, preferred_element_type=F32).astype(BF16)


def turn_kernel(terms, own_lower, mate_lower, own_upper, mate_upper, own_side, mate_side, low, out):
    groups = ((own_lower, own_upper, own_side), (mate_lower, mate_upper, mate_side))
    for slot, (lower, upper, side) in enumerate(groups):
        total = terms[0, slot].astype(F32)
        for source in range(1, terms.shape[0]):
            total += terms[source, slot].astype(F32)
        remain = (side[0].astype(F32) - total).astype(BF16)
        solved = jnp.dot(lower[0], remain, preferred_element_type=F32).astype(BF16)
        low[slot] = solved
        out[slot] = jnp.dot(upper[0], solved, preferred_element_type=F32).astype(BF16)


def level_spec(shape, level):
    return pl.BlockSpec((1,) + tuple(shape[1:]), lambda i: (level,) + (0,) * (len(shape) - 1))


def whole(shape):
    return pl.BlockSpec(tuple(shape), lambda i: (0,) * len(shape))


def small_call(kernel, arrays, levels, n_out):
    pair = jax.ShapeDtypeStruct((2,) + arrays[-1].shape[1:], BF16)
    specs = [
        whole(a.shape) if level is None else level_spec(a.shape, level)
        for a, level in zip(arrays, levels)
    ]
    outs = [pair] * n_out
    result = pl.pallas_call(
        kernel,
        grid=(1,),
        out_shape=outs,
        in_specs=specs,
        out_specs=[whole(pair.shape)] * n_out,
        compiler_params=pltpu.CompilerParams(vmem_limit_bytes=16 << 20),
    )(*arrays)
    return result


def rows_kernel(level, base, rows, per_row, step_rows, numbers, own, mate, stored, out):
    step = pl.program_id(0)
    for slot, blocks in enumerate((own, mate)):
        for r in range(step_rows):
            row = step * step_rows + r
            at = ((slot * (own_levels(numbers, rows, per_row)) + level) * rows + row) * per_row
            left = jnp.concatenate([blocks[0, r, k] for k in range(per_row)], axis=1)
            right = jnp.concatenate(
                [stored[numbers[at + k] - base] for k in range(per_row)], axis=0
            )
            out[r, slot] = jnp.dot(left, right, preferred_element_type=F32).astype(BF16)


def own_levels(numbers, rows, per_row):
    return numbers.shape[0] // (2 * rows * per_row)


def row_sums(level, base, numbers, own, mate, stored):
    _, rows, per_row, width, _ = own.shape
    step_rows = 2
    block = pl.BlockSpec(
        (1, step_rows, per_row, width, width), lambda i, n: (level, i, 0, 0, 0)
    )
    columns = stored.shape[2]
    return pl.pallas_call(
        functools.partial(rows_kernel, level, base, rows, per_row, step_rows),
        grid_spec=pltpu.PrefetchScalarGridSpec(
            num_scalar_prefetch=1,
            grid=(rows // step_rows,),
            in_specs=[block, block, pl.BlockSpec(memory_space=pltpu.VMEM)],
            out_specs=pl.BlockSpec((step_rows, 2, width, columns), lambda i, n: (i, 0, 0, 0)),
        ),
        out_shape=jax.ShapeDtypeStruct((rows, 2, width, columns), BF16),
        compiler_params=pltpu.CompilerParams(vmem_limit_bytes=24 << 20),
    )(numbers, own, mate, stored)


def shards(
    n_prow,
    right_side,
    lower_inverse,
    upper_inverse,
    lower_blocks,
    lower_index,
    upper_blocks,
    upper_index,
):
    levels, _, width, columns = right_side.shape
    half = columns // 2
    per_group = n_prow
    core = lax.rem(lax.axis_index("prow"), 2)
    mates = [(i, i ^ 1) for i in range(n_prow)]
    planes = [[i * 2 + c for i in range(n_prow // 2)] for c in range(2)]

    def swap(x):
        return lax.ppermute(x, "prow", mates)

    side = right_side[:, 0]
    parts = jnp.where(core == 0, side[:, :, :half], side[:, :, half:])
    others = jnp.where(core == 0, side[:, :, half:], side[:, :, :half])
    own_lower, own_upper = lower_inverse[:, 0], upper_inverse[:, 0]
    got = swap(jnp.concatenate([own_lower, own_upper, others], axis=0))
    mine = (own_lower, own_upper, parts)
    lower_mate, upper_mate = swap(lower_blocks), swap(upper_blocks)

    def numbers_of(index):
        both = jnp.stack([index, swap(index)])
        flipped = jnp.bitwise_xor(both, core)
        return flipped.reshape(-1)

    lower_numbers, upper_numbers = numbers_of(lower_index), numbers_of(upper_index)

    def spread(x):
        n = len(planes[0])
        sent = jnp.broadcast_to(x, (n,) + x.shape)
        heard = lax.all_to_all(sent, "prow", 0, 0, axis_index_groups=planes)
        return heard.reshape(per_group, width, half)

    def collect(x):
        return lax.all_to_all(x, "pcol", 0, 0)

    def source(kind, level):
        return [mine[kind], got], [level, kind * levels + level]

    def join(*groups):
        arrays, places = [], []
        for a, p in groups:
            arrays += a
            places += p
        return arrays, places

    a, p = join(source(0, 0), source(2, 0))
    (x,) = small_call(first_kernel, a, p, 1)
    low, pieces = [x], []
    for height in range(1, levels):
        pieces.append(spread(x))
        sums = row_sums(
            height - 1, 0, lower_numbers, lower_blocks, lower_mate, jnp.concatenate(pieces)
        )
        terms = ([collect(sums)], [None])
        if height < levels - 1:
            a, p = join(terms, source(0, height), source(2, height))
            (x,) = small_call(solve_kernel, a, p, 1)
            low.append(x)
        else:
            a, p = join(terms, source(0, height), source(1, height), source(2, height))
            _, x = small_call(turn_kernel, a, p, 2)
    solved, pieces = {levels - 1: x}, []
    for height in range(levels - 2, -1, -1):
        pieces.insert(0, spread(x))
        sums = row_sums(
            height,
            (height + 1) * per_group,
            upper_numbers,
            upper_blocks,
            upper_mate,
            jnp.concatenate(pieces),
        )
        terms = ([collect(sums)], [None])
        before = ([low[height], low[height]], [0, 1])
        a, p = join(terms, source(1, height), before)
        (x,) = small_call(solve_kernel, a, p, 1)
        solved[height] = x
    pairs = jnp.stack([solved[h] for h in range(levels)])
    kept, came = pairs[:, 0], swap(pairs[:, 1])
    first = jnp.where(core == 0, kept, came)
    second = jnp.where(core == 0, came, kept)
    return jnp.concatenate([first, second], axis=2)[:, None]


def solution(mesh):
    placed = (
        P(None, ("prow", "pcol"), None, None),
        P(None, ("prow", "pcol"), None, None),
        P(None, ("prow", "pcol"), None, None),
        P(None, "prow", "pcol", None, None),
        P(None, "prow", "pcol"),
        P(None, "prow", "pcol", None, None),
        P(None, "prow", "pcol"),
    )
    return jax.shard_map(
        functools.partial(shards, mesh.shape["prow"]),
        mesh=mesh,
        in_specs=placed,
        out_specs=P(None, ("prow", "pcol"), None, None),
        check_vma=False,
    )
```

```python
import functools

import jax
import jax.numpy as jnp
from jax import lax
from jax.experimental import pallas as pl
from jax.experimental.pallas import tpu as pltpu
from jax.sharding import PartitionSpec as P

F32 = jnp.float32
BF16 = jnp.bfloat16


def first_kernel(core, side, lower, upper, kept, mine, given):
    levels, _, width, columns = side.shape
    half = columns // 2
    here = pl.ds(pl.multiple_of(core[0] * half, half), half)
    there = pl.ds(pl.multiple_of((1 - core[0]) * half, half), half)
    for out, part in ((mine, here), (given, there)):
        for level in range(levels):
            out[level] = lower[level, 0]
            out[levels + level] = upper[level, 0]
            out[2 * levels + level] = side[level, 0, :, part]
    inverse = lower[0, 0]
    kept[...] = jnp.dot(inverse, side[0, 0, :, here], preferred_element_type=F32).astype(BF16)
    given[3 * levels] = jnp.dot(
        inverse, side[0, 0, :, there], preferred_element_type=F32
    ).astype(BF16)


def first_call(core, side, lower, upper):
    levels, _, width, columns = side.shape
    half = columns // 2
    vmem = pl.BlockSpec(memory_space=pltpu.VMEM)
    return pl.pallas_call(
        first_kernel,
        grid_spec=pltpu.PrefetchScalarGridSpec(
            num_scalar_prefetch=1,
            grid=(1,),
            in_specs=[
                pl.BlockSpec(x.shape, lambda i, c: (0, 0, 0, 0)) for x in (side, lower, upper)
            ],
            out_specs=[vmem] * 3,
        ),
        out_shape=[
            jax.ShapeDtypeStruct((width, half), BF16),
            jax.ShapeDtypeStruct((3 * levels, width, half), BF16),
            jax.ShapeDtypeStruct((3 * levels + 1, width, half), BF16),
        ],
        compiler_params=pltpu.CompilerParams(vmem_limit_bytes=16 << 20),
    )(core, side, lower, upper)


def spread_kernel(kept, got, *rest):
    out = rest[-1]
    last = got.shape[0] - 1
    for i in range(out.shape[0]):
        out[i, 0] = kept[...]
        out[i, 1] = got[last]


def spread_call(copies, kept, got, others):
    shape = (copies, 2) + kept.shape
    return pl.pallas_call(
        spread_kernel,
        in_specs=[pl.BlockSpec(memory_space=pltpu.VMEM)] * 2
        + [pl.BlockSpec(memory_space=pl.ANY)] * len(others),
        out_specs=pl.BlockSpec(memory_space=pltpu.VMEM),
        out_shape=jax.ShapeDtypeStruct(shape, BF16),
        compiler_params=pltpu.CompilerParams(vmem_limit_bytes=16 << 20),
    )(kept, got, *others)


def remain_of(terms, slot, side):
    total = terms[0, slot].astype(F32)
    for source in range(1, terms.shape[0]):
        total += terms[source, slot].astype(F32)
    return (side.astype(F32) - total).astype(BF16)


def solve_kernel(picks, terms, mine, got, *refs):
    side_pick, inverse_picks, n_before = picks
    before, outs = refs[:n_before], refs[n_before:]
    for slot, packed in enumerate((mine, got)):
        if side_pick is not None:
            side = packed[side_pick]
        elif len(before) == 1:
            side = before[0][slot]
        else:
            kept, came = before
            side = came[came.shape[0] - 1] if slot else kept[...]
        x = remain_of(terms, slot, side)
        for pick in inverse_picks:
            x = jnp.dot(packed[pick], x, preferred_element_type=F32).astype(BF16)
        outs[0][slot] = x
        for sent in outs[1:]:
            for i in range(sent.shape[0]):
                sent[i, slot] = x


def solve_call(side_pick, inverse_picks, copies, terms, mine, got, before=()):
    _, pair, width, half = terms.shape
    outs = [jax.ShapeDtypeStruct((pair, width, half), BF16)]
    if copies:
        outs.append(jax.ShapeDtypeStruct((copies, pair, width, half), BF16))
    vmem = pl.BlockSpec(memory_space=pltpu.VMEM)
    return pl.pallas_call(
        functools.partial(solve_kernel, (side_pick, inverse_picks, len(before))),
        in_specs=[vmem] * (3 + len(before)),
        out_specs=[vmem] * len(outs),
        out_shape=outs,
        compiler_params=pltpu.CompilerParams(vmem_limit_bytes=16 << 20),
    )(terms, mine, got, *before)


def rows_kernel(level, base, which, fetch, numbers, own, mate, stored, *rest):
    levels, rows, per_row = own.shape[:3]
    out = rest[-3] if fetch else rest[-1]
    if fetch:
        held, sems = rest[-2:]
        cut = rows // sems.shape[0]

        def copy(i):
            part = pl.ds(i * cut, cut)
            return pltpu.make_async_copy(own.at[level, part], held.at[part], sems.at[i])

        for i in range(sems.shape[0]):
            copy(i).start()
    for slot in (1, 0):
        if fetch and slot == 0:
            for i in range(sems.shape[0]):
                copy(i).wait()
        for row in range(rows):
            at = (((slot * 2 + which) * levels + level) * rows + row) * per_row
            if slot:
                blocks = [mate[level, row, k] for k in range(per_row)]
            elif fetch:
                blocks = [held[row, k] for k in range(per_row)]
            else:
                blocks = [own[level, row, k] for k in range(per_row)]
            left = jnp.concatenate(blocks, axis=1)
            right = jnp.concatenate(
                [stored[numbers[at + k] - base] for k in range(per_row)], axis=0
            )
            out[row, slot] = jnp.dot(left, right, preferred_element_type=F32).astype(BF16)


def row_sums(level, base, which, numbers, own, mate, stored, others=(), fetch=False):
    _, rows, per_row, width, _ = own.shape
    columns = stored.shape[2]
    vmem = pl.BlockSpec(memory_space=pltpu.VMEM)
    first, scratch = vmem, []
    if fetch:
        own = pltpu.with_memory_space_constraint(own, pltpu.HBM)
        first = pl.BlockSpec(memory_space=pltpu.HBM)
        scratch = [
            pltpu.VMEM((rows, per_row, width, width), BF16),
            pltpu.SemaphoreType.DMA((2,)),
        ]
    return pl.pallas_call(
        functools.partial(rows_kernel, level, base, which, fetch),
        grid_spec=pltpu.PrefetchScalarGridSpec(
            num_scalar_prefetch=1,
            grid=(1,),
            in_specs=[first, vmem, vmem] + [vmem] * len(others),
            out_specs=vmem,
            scratch_shapes=scratch,
        ),
        out_shape=jax.ShapeDtypeStruct((rows, 2, width, columns), BF16),
        compiler_params=pltpu.CompilerParams(vmem_limit_bytes=8 << 20),
    )(numbers, own, mate, stored, *others)


def shards(
    n_prow,
    right_side,
    lower_inverse,
    upper_inverse,
    lower_blocks,
    lower_index,
    upper_blocks,
    upper_index,
):
    levels, _, width, columns = right_side.shape
    half = columns // 2
    core = lax.rem(lax.axis_index("prow"), 2).astype(jnp.int32)
    core_ref = core.reshape(1)
    mates = [(i, i ^ 1) for i in range(n_prow)]
    planes = [[i * 2 + c for i in range(n_prow // 2)] for c in range(2)]
    copies = n_prow // 2

    def swap(x):
        return lax.ppermute(x, "prow", mates)

    small = [right_side, lower_inverse, upper_inverse]
    small = [pltpu.with_memory_space_constraint(x, pltpu.HBM) for x in small]
    kept, mine, given = first_call(core_ref, *small)
    got = swap(given)
    index = jnp.stack([lower_index, upper_index]).reshape(-1)
    index = lax.optimization_barrier(index)
    numbers = jnp.bitwise_xor(jnp.concatenate([index, swap(index)]), core)
    lower_given, upper_given, _, _ = lax.optimization_barrier(
        (lower_blocks, upper_blocks, got, numbers)
    )
    lower_mate, upper_mate = swap(lower_given), swap(upper_given)

    def heard(sent):
        got = lax.all_to_all(sent, "prow", 0, 0, axis_index_groups=planes)
        return got.reshape(n_prow, width, half)

    def collect(x):
        return lax.all_to_all(x, "pcol", 0, 0)

    sent = spread_call(copies, kept, got, [numbers])
    low, pieces = [(kept, got)], [heard(sent)]
    for height in range(1, levels):
        sums = row_sums(
            height - 1,
            0,
            0,
            numbers,
            lower_blocks,
            lower_mate,
            jnp.concatenate(pieces),
            [upper_mate] if height == 2 else [],
            height == 1,
        )
        turn = height == levels - 1
        picks = [height, levels + height] if turn else [height]
        x, sent = solve_call(2 * levels + height, picks, copies, collect(sums), mine, got)
        if not turn:
            low.append((x,))
            pieces.append(heard(sent))
    solved, pieces = {levels - 1: x}, []
    for height in range(levels - 2, -1, -1):
        pieces.insert(0, heard(sent))
        sums = row_sums(
            height,
            (height + 1) * n_prow,
            1,
            numbers,
            upper_blocks,
            upper_mate,
            jnp.concatenate(pieces),
        )
        x, *sent = solve_call(
            None,
            [levels + height],
            copies if height else 0,
            collect(sums),
            mine,
            got,
            low[height],
        )
        sent = sent[0] if sent else None
        solved[height] = x
    pairs = jnp.stack([solved[h] for h in range(levels)])
    kept, came = pairs[:, 0], swap(pairs[:, 1])
    first = jnp.where(core == 0, kept, came)
    second = jnp.where(core == 0, came, kept)
    return jnp.concatenate([first, second], axis=2)[:, None]


def solution(mesh):
    placed = (
        P(None, ("prow", "pcol"), None, None),
        P(None, ("prow", "pcol"), None, None),
        P(None, ("prow", "pcol"), None, None),
        P(None, "prow", "pcol", None, None),
        P(None, "prow", "pcol"),
        P(None, "prow", "pcol", None, None),
        P(None, "prow", "pcol"),
    )
    return jax.shard_map(
        functools.partial(shards, mesh.shape["prow"]),
        mesh=mesh,
        in_specs=placed,
        out_specs=P(None, ("prow", "pcol"), None, None),
        check_vma=False,
    )
```

```python
import functools

import jax
import jax.numpy as jnp
from jax import lax
from jax.experimental import pallas as pl
from jax.experimental.pallas import tpu as pltpu
from jax.sharding import PartitionSpec as P

F32 = jnp.float32
BF16 = jnp.bfloat16


def first_kernel(core, side, lower, upper, kept, mine, given):
    levels, _, width, columns = side.shape
    half = columns // 2
    here = pl.ds(pl.multiple_of(core[0] * half, half), half)
    there = pl.ds(pl.multiple_of((1 - core[0]) * half, half), half)
    for out, part in ((mine, here), (given, there)):
        for level in range(levels):
            out[level] = lower[level, 0]
            out[levels + level] = upper[level, 0]
            out[2 * levels + level] = side[level, 0, :, part]
    inverse = lower[0, 0]
    kept[...] = jnp.dot(inverse, side[0, 0, :, here], preferred_element_type=F32).astype(BF16)
    given[3 * levels] = jnp.dot(
        inverse, side[0, 0, :, there], preferred_element_type=F32
    ).astype(BF16)


def first_call(core, side, lower, upper):
    levels, _, width, columns = side.shape
    half = columns // 2
    vmem = pl.BlockSpec(memory_space=pltpu.VMEM)
    return pl.pallas_call(
        first_kernel,
        grid_spec=pltpu.PrefetchScalarGridSpec(
            num_scalar_prefetch=1,
            grid=(1,),
            in_specs=[
                pl.BlockSpec(x.shape, lambda i, c: (0, 0, 0, 0)) for x in (side, lower, upper)
            ],
            out_specs=[vmem] * 3,
        ),
        out_shape=[
            jax.ShapeDtypeStruct((width, half), BF16),
            jax.ShapeDtypeStruct((3 * levels, width, half), BF16),
            jax.ShapeDtypeStruct((3 * levels + 1, width, half), BF16),
        ],
        compiler_params=pltpu.CompilerParams(vmem_limit_bytes=16 << 20),
    )(core, side, lower, upper)


def spread_kernel(kept, got, *rest):
    out = rest[-1]
    last = got.shape[0] - 1
    for i in range(out.shape[0]):
        out[i, 0] = kept[...]
        out[i, 1] = got[last]


def spread_call(copies, kept, got, others):
    shape = (copies, 2) + kept.shape
    return pl.pallas_call(
        spread_kernel,
        in_specs=[pl.BlockSpec(memory_space=pltpu.VMEM)] * 2
        + [pl.BlockSpec(memory_space=pl.ANY)] * len(others),
        out_specs=pl.BlockSpec(memory_space=pltpu.VMEM),
        out_shape=jax.ShapeDtypeStruct(shape, BF16),
        compiler_params=pltpu.CompilerParams(vmem_limit_bytes=16 << 20),
    )(kept, got, *others)


def remain_of(terms, slot, side):
    total = terms[0, slot].astype(F32)
    for source in range(1, terms.shape[0]):
        total += terms[source, slot].astype(F32)
    return (side.astype(F32) - total).astype(BF16)


def solve_kernel(picks, terms, mine, got, *refs):
    side_pick, inverse_picks, n_before = picks
    before, outs = refs[:n_before], refs[n_before:]
    for slot, packed in enumerate((mine, got)):
        if side_pick is not None:
            side = packed[side_pick]
        elif len(before) == 1:
            side = before[0][slot]
        else:
            kept, came = before
            side = came[came.shape[0] - 1] if slot else kept[...]
        x = remain_of(terms, slot, side)
        for pick in inverse_picks:
            x = jnp.dot(packed[pick], x, preferred_element_type=F32).astype(BF16)
        outs[0][slot] = x
        for sent in outs[1:]:
            for i in range(sent.shape[0]):
                sent[i, slot] = x


def solve_call(side_pick, inverse_picks, copies, terms, mine, got, before=()):
    _, pair, width, half = terms.shape
    outs = [jax.ShapeDtypeStruct((pair, width, half), BF16)]
    if copies:
        outs.append(jax.ShapeDtypeStruct((copies, pair, width, half), BF16))
    vmem = pl.BlockSpec(memory_space=pltpu.VMEM)
    return pl.pallas_call(
        functools.partial(solve_kernel, (side_pick, inverse_picks, len(before))),
        in_specs=[vmem] * (3 + len(before)),
        out_specs=[vmem] * len(outs),
        out_shape=outs,
        compiler_params=pltpu.CompilerParams(vmem_limit_bytes=16 << 20),
    )(terms, mine, got, *before)


def rows_kernel(level, base, which, fetch, numbers, own, mate, stored, *rest):
    levels, rows, per_row = own.shape[:3]
    out = rest[-3] if fetch else rest[-1]
    if fetch:
        held, sems = rest[-2:]
        cut = rows // sems.shape[0]

        def copy(i):
            part = pl.ds(i * cut, cut)
            return pltpu.make_async_copy(own.at[level, part], held.at[part], sems.at[i])

        for i in range(sems.shape[0]):
            copy(i).start()
    for slot in (1, 0):
        if fetch and slot == 0:
            for i in range(sems.shape[0]):
                copy(i).wait()
        for row in range(rows):
            at = (((slot * 2 + which) * levels + level) * rows + row) * per_row
            if slot:
                blocks = [mate[level, row, k] for k in range(per_row)]
            elif fetch:
                blocks = [held[row, k] for k in range(per_row)]
            else:
                blocks = [own[level, row, k] for k in range(per_row)]
            left = jnp.concatenate(blocks, axis=1)
            right = jnp.concatenate(
                [stored[numbers[at + k] - base] for k in range(per_row)], axis=0
            )
            out[row, slot] = jnp.dot(left, right, preferred_element_type=F32).astype(BF16)


def row_sums(level, base, which, numbers, own, mate, stored, others=(), fetch=False):
    _, rows, per_row, width, _ = own.shape
    columns = stored.shape[2]
    vmem = pl.BlockSpec(memory_space=pltpu.VMEM)
    first, scratch = vmem, []
    if fetch:
        own = pltpu.with_memory_space_constraint(own, pltpu.HBM)
        first = pl.BlockSpec(memory_space=pltpu.HBM)
        scratch = [
            pltpu.VMEM((rows, per_row, width, width), BF16),
            pltpu.SemaphoreType.DMA((2,)),
        ]
    return pl.pallas_call(
        functools.partial(rows_kernel, level, base, which, fetch),
        grid_spec=pltpu.PrefetchScalarGridSpec(
            num_scalar_prefetch=1,
            grid=(1,),
            in_specs=[first, vmem, vmem] + [vmem] * len(others),
            out_specs=vmem,
            scratch_shapes=scratch,
        ),
        out_shape=jax.ShapeDtypeStruct((rows, 2, width, columns), BF16),
        compiler_params=pltpu.CompilerParams(vmem_limit_bytes=8 << 20),
    )(numbers, own, mate, stored, *others)


def shards(
    n_prow,
    right_side,
    lower_inverse,
    upper_inverse,
    lower_blocks,
    lower_index,
    upper_blocks,
    upper_index,
):
    levels, _, width, columns = right_side.shape
    half = columns // 2
    core = lax.rem(lax.axis_index("prow"), 2).astype(jnp.int32)
    core_ref = core.reshape(1)
    mates = [(i, i ^ 1) for i in range(n_prow)]
    planes = [[i * 2 + c for i in range(n_prow // 2)] for c in range(2)]
    copies = n_prow // 2
    n_pcol = lax.axis_size("pcol")
    behind = [
        (i * n_pcol + k, i * n_pcol + (k + 1) % n_pcol)
        for i in range(1, n_prow, 2)
        for k in range(n_pcol)
    ]

    def swap(x):
        return lax.ppermute(x, "prow", mates)

    small = [right_side, lower_inverse, upper_inverse]
    small = [pltpu.with_memory_space_constraint(x, pltpu.HBM) for x in small]
    kept, mine, given = first_call(core_ref, *small)
    got = swap(given)
    index = jnp.stack([lower_index, upper_index]).reshape(-1)
    index = lax.optimization_barrier(index)
    numbers = jnp.bitwise_xor(jnp.concatenate([index, swap(index)]), core)
    lower_given, upper_given, _, _ = lax.optimization_barrier(
        (lower_blocks, upper_blocks, got, numbers)
    )
    lower_mate, upper_mate = swap(lower_given), swap(upper_given)

    token = got[3 * levels, :16]
    for _ in range(5):
        token = lax.ppermute(token, ("prow", "pcol"), behind) + kept[:16]

    def heard(sent):
        got = lax.all_to_all(sent, "prow", 0, 0, axis_index_groups=planes)
        return got.reshape(n_prow, width, half)

    def collect(x):
        return lax.all_to_all(x, "pcol", 0, 0)

    sent = spread_call(copies, kept, got, [numbers, token])
    low, pieces = [(kept, got)], [heard(sent)]
    for height in range(1, levels):
        sums = row_sums(
            height - 1,
            0,
            0,
            numbers,
            lower_blocks,
            lower_mate,
            jnp.concatenate(pieces),
            [upper_mate] if height == 2 else [],
            height == 1,
        )
        turn = height == levels - 1
        picks = [height, levels + height] if turn else [height]
        x, sent = solve_call(2 * levels + height, picks, copies, collect(sums), mine, got)
        if not turn:
            low.append((x,))
            pieces.append(heard(sent))
    solved, pieces = {levels - 1: x}, []
    for height in range(levels - 2, -1, -1):
        pieces.insert(0, heard(sent))
        sums = row_sums(
            height,
            (height + 1) * n_prow,
            1,
            numbers,
            upper_blocks,
            upper_mate,
            jnp.concatenate(pieces),
        )
        x, *sent = solve_call(
            None,
            [levels + height],
            copies if height else 0,
            collect(sums),
            mine,
            got,
            low[height],
        )
        sent = sent[0] if sent else None
        solved[height] = x
    pairs = jnp.stack([solved[h] for h in range(levels)])
    kept, came = pairs[:, 0], swap(pairs[:, 1])
    first = jnp.where(core == 0, kept, came)
    second = jnp.where(core == 0, came, kept)
    return jnp.concatenate([first, second], axis=2)[:, None]


def solution(mesh):
    placed = (
        P(None, ("prow", "pcol"), None, None),
        P(None, ("prow", "pcol"), None, None),
        P(None, ("prow", "pcol"), None, None),
        P(None, "prow", "pcol", None, None),
        P(None, "prow", "pcol"),
        P(None, "prow", "pcol", None, None),
        P(None, "prow", "pcol"),
    )
    return jax.shard_map(
        functools.partial(shards, mesh.shape["prow"]),
        mesh=mesh,
        in_specs=placed,
        out_specs=P(None, ("prow", "pcol"), None, None),
        check_vma=False,
    )
```

```python
import functools

import jax
import jax.numpy as jnp
from jax import lax
from jax.experimental import pallas as pl
from jax.experimental.pallas import tpu as pltpu
from jax.sharding import PartitionSpec as P

F32 = jnp.float32
BF16 = jnp.bfloat16


def first_kernel(core, side, lower, upper, blocks, mine, given, near, *scratch):
    levels, _, width, columns = side.shape
    held, sems = scratch[:3], scratch[3]
    half = columns // 2
    cut = near.shape[1] // 2

    def copy(i):
        if i < 3:
            return pltpu.make_async_copy((side, lower, upper)[i], held[i], sems.at[i])
        part = pl.ds((i - 3) * cut, cut)
        return pltpu.make_async_copy(blocks.at[0, part], near.at[0, part], sems.at[i])

    for i in range(5):
        copy(i).start()
    for i in range(3):
        copy(i).wait()
    here = pl.ds(pl.multiple_of(core[0] * half, half), half)
    there = pl.ds(pl.multiple_of((1 - core[0]) * half, half), half)
    sides, lowers, uppers = held
    for out, part in ((given, there), (mine, here)):
        for level in range(levels):
            out[level] = lowers[level, 0]
            out[levels + level] = uppers[level, 0]
            out[2 * levels + level] = sides[level, 0, :, part]
        out[3 * levels] = jnp.dot(
            lowers[0, 0], sides[0, 0, :, part], preferred_element_type=F32
        ).astype(BF16)
    for i in range(3, 5):
        copy(i).wait()


def first_call(core, *arrays):
    levels, _, width, columns = arrays[0].shape
    packed = jax.ShapeDtypeStruct((3 * levels + 1, width, columns // 2), BF16)
    near = jax.ShapeDtypeStruct((1,) + arrays[3].shape[1:], BF16)
    arrays = [pltpu.with_memory_space_constraint(x, pltpu.HBM) for x in arrays]
    return pl.pallas_call(
        first_kernel,
        grid_spec=pltpu.PrefetchScalarGridSpec(
            num_scalar_prefetch=1,
            grid=(1,),
            in_specs=[pl.BlockSpec(memory_space=pltpu.HBM)] * 4,
            out_specs=[pl.BlockSpec(memory_space=pltpu.VMEM)] * 3,
            scratch_shapes=[pltpu.VMEM(x.shape, BF16) for x in arrays[:3]]
            + [pltpu.SemaphoreType.DMA((5,))],
        ),
        out_shape=[packed, packed, near],
        compiler_params=pltpu.CompilerParams(vmem_limit_bytes=16 << 20),
    )(core, *arrays)


def spread_kernel(mine, got, *rest):
    out = rest[-1]
    last = got.shape[0] - 1
    for i in range(out.shape[0]):
        out[i, 0] = mine[last]
        out[i, 1] = got[last]


def spread_call(copies, mine, got, others):
    shape = (copies, 2) + got.shape[1:]
    return pl.pallas_call(
        spread_kernel,
        in_specs=[pl.BlockSpec(memory_space=pltpu.VMEM)] * 2
        + [pl.BlockSpec(memory_space=pl.ANY)] * len(others),
        out_specs=pl.BlockSpec(memory_space=pltpu.VMEM),
        out_shape=jax.ShapeDtypeStruct(shape, BF16),
        compiler_params=pltpu.CompilerParams(vmem_limit_bytes=16 << 20),
    )(mine, got, *others)


def remain_of(terms, slot, side):
    total = terms[0, slot].astype(F32)
    for source in range(1, terms.shape[0]):
        total += terms[source, slot].astype(F32)
    return (side.astype(F32) - total).astype(BF16)


def solve_kernel(picks, terms, mine, got, *refs):
    side_pick, inverse_picks, n_before = picks
    before, outs = refs[:n_before], refs[n_before:]
    for slot, packed in enumerate((mine, got)):
        side = before[0][slot] if before else packed[side_pick]
        x = remain_of(terms, slot, side)
        for pick in inverse_picks:
            x = jnp.dot(packed[pick], x, preferred_element_type=F32).astype(BF16)
        outs[0][slot] = x
        for sent in outs[1:]:
            for i in range(sent.shape[0]):
                sent[i, slot] = x


def solve_call(side_pick, inverse_picks, copies, terms, mine, got, before=()):
    _, pair, width, half = terms.shape
    outs = [jax.ShapeDtypeStruct((pair, width, half), BF16)]
    if copies:
        outs.append(jax.ShapeDtypeStruct((copies, pair, width, half), BF16))
    vmem = pl.BlockSpec(memory_space=pltpu.VMEM)
    return pl.pallas_call(
        functools.partial(solve_kernel, (side_pick, inverse_picks, len(before))),
        in_specs=[vmem] * (3 + len(before)),
        out_specs=[vmem] * len(outs),
        out_shape=outs,
        compiler_params=pltpu.CompilerParams(vmem_limit_bytes=16 << 20),
    )(terms, mine, got, *before)


def rows_kernel(level, base, which, numbers, own, mate, stored, *rest):
    levels, rows, per_row = mate.shape[:3]
    out = rest[-1]
    for slot, blocks in enumerate((own, mate)):
        at_level = level if blocks.shape[0] == levels else 0
        for row in range(rows):
            at = (((slot * 2 + which) * levels + level) * rows + row) * per_row
            left = jnp.concatenate([blocks[at_level, row, k] for k in range(per_row)], axis=1)
            right = jnp.concatenate(
                [stored[numbers[at + k] - base] for k in range(per_row)], axis=0
            )
            out[row, slot] = jnp.dot(left, right, preferred_element_type=F32).astype(BF16)


def row_sums(level, base, which, numbers, own, mate, stored, others=()):
    _, rows, per_row, width, _ = own.shape
    vmem = pl.BlockSpec(memory_space=pltpu.VMEM)
    return pl.pallas_call(
        functools.partial(rows_kernel, level, base, which),
        grid_spec=pltpu.PrefetchScalarGridSpec(
            num_scalar_prefetch=1,
            grid=(1,),
            in_specs=[vmem] * (3 + len(others)),
            out_specs=vmem,
        ),
        out_shape=jax.ShapeDtypeStruct((rows, 2, width, stored.shape[2]), BF16),
        compiler_params=pltpu.CompilerParams(vmem_limit_bytes=8 << 20),
    )(numbers, own, mate, stored, *others)


def shards(
    n_prow,
    right_side,
    lower_inverse,
    upper_inverse,
    lower_blocks,
    lower_index,
    upper_blocks,
    upper_index,
):
    levels, _, width, columns = right_side.shape
    half = columns // 2
    core = lax.rem(lax.axis_index("prow"), 2).astype(jnp.int32)
    core_ref = core.reshape(1)
    mates = [(i, i ^ 1) for i in range(n_prow)]
    planes = [[i * 2 + c for i in range(n_prow // 2)] for c in range(2)]
    copies = n_prow // 2
    n_pcol = lax.axis_size("pcol")
    behind = [
        (i * n_pcol + k, i * n_pcol + (k + 3) % n_pcol)
        for i in range(1, n_prow, 2)
        for k in range(n_pcol)
    ]

    def swap(x):
        return lax.ppermute(x, "prow", mates)

    index = [lower_index, upper_index]
    index = jnp.stack(index + [swap(x) for x in index])
    mine, given, near = first_call(
        core_ref, right_side, lower_inverse, upper_inverse, lower_blocks
    )
    got = swap(given)
    numbers = jnp.bitwise_xor(index, core).reshape(-1)
    lower_given, upper_given, _, _ = lax.optimization_barrier(
        (lower_blocks, upper_blocks, got, numbers)
    )
    lower_mate, upper_mate = swap(lower_given), swap(upper_given)

    token = mine
    for _ in range(1):
        token = lax.ppermute(token, ("prow", "pcol"), behind)

    def heard(sent):
        got = lax.all_to_all(sent, "prow", 0, 0, axis_index_groups=planes)
        return got.reshape(n_prow, width, half)

    def collect(x):
        return lax.all_to_all(x, "pcol", 0, 0)

    sent = spread_call(copies, mine, got, [numbers, token])
    low, pieces = [()], [heard(sent)]
    for height in range(1, levels):
        sums = row_sums(
            height - 1,
            0,
            0,
            numbers,
            near if height == 1 else lower_blocks,
            lower_mate,
            jnp.concatenate(pieces),
            [upper_mate] if height == 2 else [],
        )
        turn = height == levels - 1
        picks = [height, levels + height] if turn else [height]
        x, sent = solve_call(2 * levels + height, picks, copies, collect(sums), mine, got)
        if not turn:
            low.append((x,))
            pieces.append(heard(sent))
    solved, pieces = {levels - 1: x}, []
    for height in range(levels - 2, -1, -1):
        pieces.insert(0, heard(sent))
        sums = row_sums(
            height,
            (height + 1) * n_prow,
            1,
            numbers,
            upper_blocks,
            upper_mate,
            jnp.concatenate(pieces),
        )
        x, *sent = solve_call(
            3 * levels,
            [levels + height],
            copies if height else 0,
            collect(sums),
            mine,
            got,
            low[height],
        )
        sent = sent[0] if sent else None
        solved[height] = x
    pairs = jnp.stack([solved[h] for h in range(levels)])
    kept, came = pairs[:, 0], swap(pairs[:, 1])
    first = jnp.where(core == 0, kept, came)
    second = jnp.where(core == 0, came, kept)
    return jnp.concatenate([first, second], axis=2)[:, None]


def solution(mesh):
    placed = (
        P(None, ("prow", "pcol"), None, None),
        P(None, ("prow", "pcol"), None, None),
        P(None, ("prow", "pcol"), None, None),
        P(None, "prow", "pcol", None, None),
        P(None, "prow", "pcol"),
        P(None, "prow", "pcol", None, None),
        P(None, "prow", "pcol"),
    )
    return jax.shard_map(
        functools.partial(shards, mesh.shape["prow"]),
        mesh=mesh,
        in_specs=placed,
        out_specs=P(None, ("prow", "pcol"), None, None),
        check_vma=False,
    )
```

```python
import functools

import jax
import jax.numpy as jnp
from jax import lax
from jax.experimental import pallas as pl
from jax.experimental.pallas import tpu as pltpu
from jax.sharding import PartitionSpec as P

F32 = jnp.float32
BF16 = jnp.bfloat16


def first_kernel(core, side, lower, upper, blocks, mine, given, near, *scratch):
    levels, _, width, columns = side.shape
    held, sems = scratch[:3], scratch[3]
    half = columns // 2
    cut = near.shape[1] // 2

    def copy(i):
        if i < 3:
            return pltpu.make_async_copy((side, lower, upper)[i], held[i], sems.at[i])
        part = pl.ds((i - 3) * cut, cut)
        return pltpu.make_async_copy(blocks.at[0, part], near.at[0, part], sems.at[i])

    for i in range(5):
        copy(i).start()
    for i in range(3):
        copy(i).wait()
    here = pl.ds(pl.multiple_of(core[0] * half, half), half)
    there = pl.ds(pl.multiple_of((1 - core[0]) * half, half), half)
    sides, lowers, uppers = held
    for out, part in ((given, there), (mine, here)):
        for level in range(levels):
            out[level] = lowers[level, 0]
            out[levels + level] = uppers[level, 0]
            out[2 * levels + level] = sides[level, 0, :, part]
        out[3 * levels] = jnp.dot(
            lowers[0, 0], sides[0, 0, :, part], preferred_element_type=F32
        ).astype(BF16)
        out[3 * levels + 1] = out[3 * levels]
        out[3 * levels + 2] = out[3 * levels]
    for i in range(3, 5):
        copy(i).wait()


def first_call(core, *arrays):
    levels, _, width, columns = arrays[0].shape
    packed = jax.ShapeDtypeStruct((3 * levels + 3, width, columns // 2), BF16)
    near = jax.ShapeDtypeStruct((1,) + arrays[3].shape[1:], BF16)
    arrays = [pltpu.with_memory_space_constraint(x, pltpu.HBM) for x in arrays]
    return pl.pallas_call(
        first_kernel,
        grid_spec=pltpu.PrefetchScalarGridSpec(
            num_scalar_prefetch=1,
            grid=(1,),
            in_specs=[pl.BlockSpec(memory_space=pltpu.HBM)] * 4,
            out_specs=[pl.BlockSpec(memory_space=pltpu.VMEM)] * 3,
            scratch_shapes=[pltpu.VMEM(x.shape, BF16) for x in arrays[:3]]
            + [pltpu.SemaphoreType.DMA((5,))],
        ),
        out_shape=[packed, packed, near],
        compiler_params=pltpu.CompilerParams(vmem_limit_bytes=16 << 20),
    )(core, *arrays)


def spread_kernel(mine, got, *rest):
    out = rest[-1]
    last = got.shape[0] - 1
    for i in range(out.shape[0]):
        out[i, 0] = mine[last]
        out[i, 1] = got[last]


def spread_call(copies, mine, got, others):
    shape = (copies, 2) + got.shape[1:]
    return pl.pallas_call(
        spread_kernel,
        in_specs=[pl.BlockSpec(memory_space=pltpu.VMEM)] * 2
        + [pl.BlockSpec(memory_space=pl.ANY)] * len(others),
        out_specs=pl.BlockSpec(memory_space=pltpu.VMEM),
        out_shape=jax.ShapeDtypeStruct(shape, BF16),
        compiler_params=pltpu.CompilerParams(vmem_limit_bytes=16 << 20),
    )(mine, got, *others)


def remain_of(terms, slot, side):
    total = terms[0, slot].astype(F32)
    for source in range(1, terms.shape[0]):
        total += terms[source, slot].astype(F32)
    return (side.astype(F32) - total).astype(BF16)


def solve_kernel(picks, terms, mine, got, *refs):
    side_pick, inverse_picks, n_before = picks
    before, outs = refs[:n_before], refs[n_before:]
    for slot, packed in enumerate((mine, got)):
        side = before[0][slot] if before else packed[side_pick]
        x = remain_of(terms, slot, side)
        for pick in inverse_picks:
            x = jnp.dot(packed[pick], x, preferred_element_type=F32).astype(BF16)
        outs[0][slot] = x
        for sent in outs[1:]:
            for i in range(sent.shape[0]):
                sent[i, slot] = x


def solve_call(side_pick, inverse_picks, copies, terms, mine, got, before=()):
    _, pair, width, half = terms.shape
    outs = [jax.ShapeDtypeStruct((pair, width, half), BF16)]
    if copies:
        outs.append(jax.ShapeDtypeStruct((copies, pair, width, half), BF16))
    vmem = pl.BlockSpec(memory_space=pltpu.VMEM)
    return pl.pallas_call(
        functools.partial(solve_kernel, (side_pick, inverse_picks, len(before))),
        in_specs=[vmem] * (3 + len(before)),
        out_specs=[vmem] * len(outs),
        out_shape=outs,
        compiler_params=pltpu.CompilerParams(vmem_limit_bytes=16 << 20),
    )(terms, mine, got, *before)


def rows_kernel(level, base, which, numbers, own, mate, stored, *rest):
    levels, rows, per_row = mate.shape[:3]
    out = rest[-1]
    for slot, blocks in enumerate((own, mate)):
        at_level = level if blocks.shape[0] == levels else 0
        for row in range(rows):
            at = (((slot * 2 + which) * levels + level) * rows + row) * per_row
            left = jnp.concatenate([blocks[at_level, row, k] for k in range(per_row)], axis=1)
            right = jnp.concatenate(
                [stored[numbers[at + k] - base] for k in range(per_row)], axis=0
            )
            out[row, slot] = jnp.dot(left, right, preferred_element_type=F32).astype(BF16)


def row_sums(level, base, which, numbers, own, mate, stored, others=()):
    _, rows, per_row, width, _ = own.shape
    vmem = pl.BlockSpec(memory_space=pltpu.VMEM)
    return pl.pallas_call(
        functools.partial(rows_kernel, level, base, which),
        grid_spec=pltpu.PrefetchScalarGridSpec(
            num_scalar_prefetch=1,
            grid=(1,),
            in_specs=[vmem] * (3 + len(others)),
            out_specs=vmem,
        ),
        out_shape=jax.ShapeDtypeStruct((rows, 2, width, stored.shape[2]), BF16),
        compiler_params=pltpu.CompilerParams(vmem_limit_bytes=8 << 20),
    )(numbers, own, mate, stored, *others)


def shards(
    n_prow,
    right_side,
    lower_inverse,
    upper_inverse,
    lower_blocks,
    lower_index,
    upper_blocks,
    upper_index,
):
    levels, _, width, columns = right_side.shape
    half = columns // 2
    core = lax.rem(lax.axis_index("prow"), 2).astype(jnp.int32)
    core_ref = core.reshape(1)
    mates = [(i, i ^ 1) for i in range(n_prow)]
    planes = [[i * 2 + c for i in range(n_prow // 2)] for c in range(2)]
    copies = n_prow // 2
    n_pcol = lax.axis_size("pcol")
    behind = [
        (i * n_pcol + k, i * n_pcol + (k + 3) % n_pcol)
        for i in range(1, n_prow, 2)
        for k in range(n_pcol)
    ]

    def swap(x):
        return lax.ppermute(x, "prow", mates)

    index = [lower_index, upper_index]
    index = jnp.stack(index + [swap(x) for x in index])
    mine, given, near = first_call(
        core_ref, right_side, lower_inverse, upper_inverse, lower_blocks
    )
    got = swap(given)
    numbers = jnp.bitwise_xor(index, core).reshape(-1)
    lower_given, upper_given, _, _ = lax.optimization_barrier(
        (lower_blocks, upper_blocks, got, numbers)
    )
    lower_mate, upper_mate = swap(lower_given), swap(upper_given)

    token = mine
    for _ in range(1):
        token = lax.ppermute(token, ("prow", "pcol"), behind)

    def heard(sent):
        got = lax.all_to_all(sent, "prow", 0, 0, axis_index_groups=planes)
        return got.reshape(n_prow, width, half)

    def collect(x):
        return lax.all_to_all(x, "pcol", 0, 0)

    sent = spread_call(copies, mine, got, [numbers, token])
    low, pieces = [()], [heard(sent)]
    for height in range(1, levels):
        sums = row_sums(
            height - 1,
            0,
            0,
            numbers,
            near if height == 1 else lower_blocks,
            lower_mate,
            jnp.concatenate(pieces),
            [upper_mate] if height == 2 else [],
        )
        turn = height == levels - 1
        picks = [height, levels + height] if turn else [height]
        x, sent = solve_call(2 * levels + height, picks, copies, collect(sums), mine, got)
        if not turn:
            low.append((x,))
            pieces.append(heard(sent))
    solved, pieces = {levels - 1: x}, []
    for height in range(levels - 2, -1, -1):
        pieces.insert(0, heard(sent))
        sums = row_sums(
            height,
            (height + 1) * n_prow,
            1,
            numbers,
            upper_blocks,
            upper_mate,
            jnp.concatenate(pieces),
        )
        x, *sent = solve_call(
            3 * levels,
            [levels + height],
            copies if height else 0,
            collect(sums),
            mine,
            got,
            low[height],
        )
        sent = sent[0] if sent else None
        solved[height] = x
    pairs = jnp.stack([solved[h] for h in range(levels)])
    kept, came = pairs[:, 0], swap(pairs[:, 1])
    first = jnp.where(core == 0, kept, came)
    second = jnp.where(core == 0, came, kept)
    return jnp.concatenate([first, second], axis=2)[:, None]


def solution(mesh):
    placed = (
        P(None, ("prow", "pcol"), None, None),
        P(None, ("prow", "pcol"), None, None),
        P(None, ("prow", "pcol"), None, None),
        P(None, "prow", "pcol", None, None),
        P(None, "prow", "pcol"),
        P(None, "prow", "pcol", None, None),
        P(None, "prow", "pcol"),
    )
    return jax.shard_map(
        functools.partial(shards, mesh.shape["prow"]),
        mesh=mesh,
        in_specs=placed,
        out_specs=P(None, ("prow", "pcol"), None, None),
        check_vma=False,
    )
```

```python
import functools

import jax
import jax.numpy as jnp
from jax import lax
from jax.experimental import pallas as pl
from jax.experimental.pallas import tpu as pltpu
from jax.sharding import PartitionSpec as P

F32 = jnp.float32
BF16 = jnp.bfloat16


def first_kernel(core, side, lower, upper, blocks, mine, given, near, *scratch):
    levels, _, width, columns = side.shape
    held, sems = scratch[:3], scratch[3]
    half = columns // 2
    cut = near.shape[1] // 2

    def copy(i):
        if i < 3:
            return pltpu.make_async_copy((side, lower, upper)[i], held[i], sems.at[i])
        part = pl.ds((i - 3) * cut, cut)
        return pltpu.make_async_copy(blocks.at[0, part], near.at[0, part], sems.at[i])

    for i in range(5):
        copy(i).start()
    for i in range(3):
        copy(i).wait()
    here = pl.ds(pl.multiple_of(core[0] * half, half), half)
    there = pl.ds(pl.multiple_of((1 - core[0]) * half, half), half)
    sides, lowers, uppers = held
    for out, part in ((given, there), (mine, here)):
        for level in range(levels):
            out[level] = lowers[level, 0]
            out[levels + level] = uppers[level, 0]
            out[2 * levels + level] = sides[level, 0, :, part]
        out[3 * levels] = jnp.dot(
            lowers[0, 0], sides[0, 0, :, part], preferred_element_type=F32
        ).astype(BF16)
        for row in range(3 * levels + 1, out.shape[0]):
            out[row] = out[3 * levels]
    for i in range(3, 5):
        copy(i).wait()


def first_call(core, *arrays):
    levels, _, width, columns = arrays[0].shape
    packed = jax.ShapeDtypeStruct((3 * levels + 1, width, columns // 2), BF16)
    longer = jax.ShapeDtypeStruct((3 * levels + 3, width, columns // 2), BF16)
    near = jax.ShapeDtypeStruct((1,) + arrays[3].shape[1:], BF16)
    arrays = [pltpu.with_memory_space_constraint(x, pltpu.HBM) for x in arrays]
    return pl.pallas_call(
        first_kernel,
        grid_spec=pltpu.PrefetchScalarGridSpec(
            num_scalar_prefetch=1,
            grid=(1,),
            in_specs=[pl.BlockSpec(memory_space=pltpu.HBM)] * 4,
            out_specs=[pl.BlockSpec(memory_space=pltpu.VMEM)] * 3,
            scratch_shapes=[pltpu.VMEM(x.shape, BF16) for x in arrays[:3]]
            + [pltpu.SemaphoreType.DMA((5,))],
        ),
        out_shape=[longer, packed, near],
        compiler_params=pltpu.CompilerParams(vmem_limit_bytes=16 << 20),
    )(core, *arrays)


def spread_kernel(mine, got, *rest):
    out = rest[-1]
    last = got.shape[0] - 1
    for i in range(out.shape[0]):
        out[i, 0] = mine[last]
        out[i, 1] = got[last]


def spread_call(copies, mine, got, others):
    shape = (copies, 2) + got.shape[1:]
    return pl.pallas_call(
        spread_kernel,
        in_specs=[pl.BlockSpec(memory_space=pltpu.VMEM)] * 2
        + [pl.BlockSpec(memory_space=pl.ANY)] * len(others),
        out_specs=pl.BlockSpec(memory_space=pltpu.VMEM),
        out_shape=jax.ShapeDtypeStruct(shape, BF16),
        compiler_params=pltpu.CompilerParams(vmem_limit_bytes=16 << 20),
    )(mine, got, *others)


def remain_of(terms, slot, side):
    total = terms[0, slot].astype(F32)
    for source in range(1, terms.shape[0]):
        total += terms[source, slot].astype(F32)
    return (side.astype(F32) - total).astype(BF16)


def solve_kernel(picks, terms, mine, got, *refs):
    side_pick, inverse_picks, n_before = picks
    before, outs = refs[:n_before], refs[n_before:]
    for slot, packed in enumerate((mine, got)):
        side = before[0][slot] if before else packed[side_pick]
        x = remain_of(terms, slot, side)
        for pick in inverse_picks:
            x = jnp.dot(packed[pick], x, preferred_element_type=F32).astype(BF16)
        outs[0][slot] = x
        for sent in outs[1:]:
            for i in range(sent.shape[0]):
                sent[i, slot] = x


def solve_call(side_pick, inverse_picks, copies, terms, mine, got, before=()):
    _, pair, width, half = terms.shape
    outs = [jax.ShapeDtypeStruct((pair, width, half), BF16)]
    if copies:
        outs.append(jax.ShapeDtypeStruct((copies, pair, width, half), BF16))
    vmem = pl.BlockSpec(memory_space=pltpu.VMEM)
    return pl.pallas_call(
        functools.partial(solve_kernel, (side_pick, inverse_picks, len(before))),
        in_specs=[vmem] * (3 + len(before)),
        out_specs=[vmem] * len(outs),
        out_shape=outs,
        compiler_params=pltpu.CompilerParams(vmem_limit_bytes=16 << 20),
    )(terms, mine, got, *before)


def rows_kernel(level, base, which, numbers, own, mate, stored, *rest):
    levels, rows, per_row = mate.shape[:3]
    out = rest[-1]
    for slot, blocks in enumerate((own, mate)):
        at_level = level if blocks.shape[0] == levels else 0
        for row in range(rows):
            at = (((slot * 2 + which) * levels + level) * rows + row) * per_row
            left = jnp.concatenate([blocks[at_level, row, k] for k in range(per_row)], axis=1)
            right = jnp.concatenate(
                [stored[numbers[at + k] - base] for k in range(per_row)], axis=0
            )
            out[row, slot] = jnp.dot(left, right, preferred_element_type=F32).astype(BF16)


def row_sums(level, base, which, numbers, own, mate, stored, others=()):
    _, rows, per_row, width, _ = own.shape
    vmem = pl.BlockSpec(memory_space=pltpu.VMEM)
    return pl.pallas_call(
        functools.partial(rows_kernel, level, base, which),
        grid_spec=pltpu.PrefetchScalarGridSpec(
            num_scalar_prefetch=1,
            grid=(1,),
            in_specs=[vmem] * (3 + len(others)),
            out_specs=vmem,
        ),
        out_shape=jax.ShapeDtypeStruct((rows, 2, width, stored.shape[2]), BF16),
        compiler_params=pltpu.CompilerParams(vmem_limit_bytes=8 << 20),
    )(numbers, own, mate, stored, *others)


def shards(
    n_prow,
    right_side,
    lower_inverse,
    upper_inverse,
    lower_blocks,
    lower_index,
    upper_blocks,
    upper_index,
):
    levels, _, width, columns = right_side.shape
    half = columns // 2
    core = lax.rem(lax.axis_index("prow"), 2).astype(jnp.int32)
    core_ref = core.reshape(1)
    mates = [(i, i ^ 1) for i in range(n_prow)]
    planes = [[i * 2 + c for i in range(n_prow // 2)] for c in range(2)]
    copies = n_prow // 2
    n_pcol = lax.axis_size("pcol")
    behind = [
        (i * n_pcol + k, i * n_pcol + (k + 3) % n_pcol)
        for i in range(1, n_prow, 2)
        for k in range(n_pcol)
    ]

    def swap(x):
        return lax.ppermute(x, "prow", mates)

    index = [lower_index, upper_index]
    index = jnp.stack(index + [swap(x) for x in index])
    mine, given, near = first_call(
        core_ref, right_side, lower_inverse, upper_inverse, lower_blocks
    )
    got = swap(given)
    numbers = jnp.bitwise_xor(index, core).reshape(-1)
    lower_given, upper_given, _, _ = lax.optimization_barrier(
        (lower_blocks, upper_blocks, got, numbers)
    )
    lower_mate, upper_mate = swap(lower_given), swap(upper_given)

    token = mine
    for _ in range(1):
        token = lax.ppermute(token, ("prow", "pcol"), behind)

    def heard(sent):
        got = lax.all_to_all(sent, "prow", 0, 0, axis_index_groups=planes)
        return got.reshape(n_prow, width, half)

    def collect(x):
        return lax.all_to_all(x, "pcol", 0, 0)

    sent = spread_call(copies, mine, got, [numbers, token])
    low, pieces = [()], [heard(sent)]
    for height in range(1, levels):
        sums = row_sums(
            height - 1,
            0,
            0,
            numbers,
            near if height == 1 else lower_blocks,
            lower_mate,
            jnp.concatenate(pieces),
            [upper_mate] if height == 2 else [],
        )
        turn = height == levels - 1
        picks = [height, levels + height] if turn else [height]
        x, sent = solve_call(2 * levels + height, picks, copies, collect(sums), mine, got)
        if not turn:
            low.append((x,))
            pieces.append(heard(sent))
    solved, pieces = {levels - 1: x}, []
    for height in range(levels - 2, -1, -1):
        pieces.insert(0, heard(sent))
        sums = row_sums(
            height,
            (height + 1) * n_prow,
            1,
            numbers,
            upper_blocks,
            upper_mate,
            jnp.concatenate(pieces),
        )
        x, *sent = solve_call(
            3 * levels,
            [levels + height],
            copies if height else 0,
            collect(sums),
            mine,
            got,
            low[height],
        )
        sent = sent[0] if sent else None
        solved[height] = x
    pairs = jnp.stack([solved[h] for h in range(levels)])
    kept, came = pairs[:, 0], swap(pairs[:, 1])
    first = jnp.where(core == 0, kept, came)
    second = jnp.where(core == 0, came, kept)
    return jnp.concatenate([first, second], axis=2)[:, None]


def solution(mesh):
    placed = (
        P(None, ("prow", "pcol"), None, None),
        P(None, ("prow", "pcol"), None, None),
        P(None, ("prow", "pcol"), None, None),
        P(None, "prow", "pcol", None, None),
        P(None, "prow", "pcol"),
        P(None, "prow", "pcol", None, None),
        P(None, "prow", "pcol"),
    )
    return jax.shard_map(
        functools.partial(shards, mesh.shape["prow"]),
        mesh=mesh,
        in_specs=placed,
        out_specs=P(None, ("prow", "pcol"), None, None),
        check_vma=False,
    )
```
